32 devices in a mesh: groups: 2 (over x), tile: 16 (over z, y, core).
Axes of the slice: x: 2, y: 2, z: 4, core: 2. Of those that a mesh axis runs over, the one named last changes fastest.
Arguments:
- features: bfloat16 [2, 192, 160, 256], P('groups', 'tile'), parts along dimension 0, may hold values from -6 to 6
- cotangent: bfloat16 [2, 192, 160, 256], P('groups', 'tile'), parts along dimension 0, may hold values from -6 to 6
- weight_one: bfloat16 [256, 9, 256], replicated, may hold values from -0.125 to 0.125
- weight_two: bfloat16 [256, 9, 256], replicated, may hold values from -0.125 to 0.125
Outputs:
- block_out: bfloat16 [2, 192, 160, 256], P('groups', 'tile'), parts along dimension 0
- input_grad: bfloat16 [2, 192, 160, 256], P('groups', 'tile'), parts along dimension 0
- grad_one: float32 [256, 18, 256], P('tile', 'groups'), parts along dimension 1
- grad_two: float32 [256, 18, 256], P('tile', 'groups'), parts along dimension 1
The draws below stay inside these ranges and needn't reach their ends.
There are 2 independent parts, one for each index of `groups`. The reference program is written for one: setup_inputs(seed, part) draws one part's arguments, and reference() takes and returns one part's arrays. A program takes and returns all parts, laid end to end along the dimension named above; an argument that names none is the same for every part. Nothing has to cross between parts.
All inputs are finite; a program needn't handle non-finite values.
Results may differ from the reference program's by a relative error of at most 0.0032.
Values may be sent and summed in bfloat16 or wider, within the bound.
A program may use at most 128 MiB of HBM per device.

```python
import jax
import jax.numpy as jnp

C = 256
MB = 1
W = 160
NH = 192


def spiked(drawn, key, source, target, shards_of, factor):
    def block_of(axis_at):
        return (jnp.arange(drawn.shape[axis_at]) // (drawn.shape[axis_at] // shards_of)).reshape((-1,) + (1,) * (drawn.ndim - 1 - axis_at))

    near = jax.random.permutation(key, shards_of)[block_of(target)]
    other_side = (block_of(target) + shards_of // 2) % shards_of
    return jnp.where((block_of(source) == near) | (block_of(source) == other_side), factor * drawn, drawn)


def levels(own_key, shape, split, low, high):
    factor_of, own = 1.0, jax.random.fold_in(own_key, 6)
    for position, shards_of in split:
        steps = jnp.exp(jax.random.uniform(jax.random.fold_in(own, position), (shards_of,), jnp.float32, low / len(split), high / len(split)))
        factor_of = factor_of * jnp.repeat(steps, shape[position] // shards_of).reshape([-1 if axis == position else 1 for axis in range(len(shape))])
    return factor_of


def bell_draw(stream_key, dims, width, most, pieces=(), kind=jnp.bfloat16):
    values = width * jax.random.normal(stream_key, dims, jnp.float32)
    if pieces:
        values = values * levels(stream_key, dims, pieces, -0.22, 0.18)
    return jnp.clip(values, -most, most).astype(kind)


def gaussian_with(key, shape, scale, bound, split, heavy, dtype=jnp.bfloat16):
    drawn = scale * jax.random.normal(key, shape, jnp.float32)
    if split:
        drawn = drawn * levels(key, shape, split, -0.22, 0.18)
    return jnp.clip(spiked(drawn, jax.random.fold_in(key, 3), *heavy), -bound, bound).astype(dtype)


def setup_inputs(seed: int = 0, part: int = 0) -> dict:
    keys = jax.random.split(jax.random.key(seed), 5)
    own_keys = jax.random.split(jax.random.fold_in(keys[4], part), 5)
    features = gaussian_with(own_keys[0], (MB, NH, W, C), 1.0, 6.0, ((1, 16),), (1, 3, 16, 2.0))
    cotangent = bell_draw(own_keys[1], (MB, NH, W, C), 1.0, 6.0, ((1, 16),))
    weight_one = bell_draw(keys[2], (C, 9, C), (9 * C) ** -0.5, 0.125)
    weight_two = bell_draw(keys[3], (C, 9, C), (9 * C) ** -0.5, 0.125)
    return {"features": features, "cotangent": cotangent, "weight_one": weight_one, "weight_two": weight_two}


def pad_field(field):
    return jnp.pad(field.astype(jnp.float32), ((0, 0), (1, 1), (1, 1), (0, 0)))

def window(padded, tap_index, row_count, col_count, direction):
    row_shift = direction * (tap_index // 3 - 1)
    col_shift = direction * (tap_index % 3 - 1)
    return padded[:, 1 + row_shift:1 + row_shift + row_count, 1 + col_shift:1 + col_shift + col_count, :]

def conv_forward(field, kernel):
    padded = pad_field(field)
    kernel_f = kernel.astype(jnp.float32)
    total = jnp.zeros(field.shape, jnp.float32)
    for tap_index in range(9):
        piece = window(padded, tap_index, field.shape[1], field.shape[2], 1)
        total = total + jnp.einsum('brwi,io->brwo', piece, kernel_f[:, tap_index, :])
    return total

def conv_transpose(field, kernel):
    padded = pad_field(field)
    kernel_f = kernel.astype(jnp.float32)
    total = jnp.zeros(field.shape, jnp.float32)
    for tap_index in range(9):
        piece = window(padded, tap_index, field.shape[1], field.shape[2], -1)
        total = total + jnp.einsum('brwo,io->brwi', piece, kernel_f[:, tap_index, :])
    return total

def kernel_grad(source, grad):
    padded = pad_field(source)
    grad_f = grad.astype(jnp.float32)
    taps = []
    for tap_index in range(9):
        piece = window(padded, tap_index, source.shape[1], source.shape[2], 1)
        taps.append(jnp.einsum('brwi,brwo->io', piece, grad_f))
    return jnp.stack(taps, axis=1)

def reference(features, cotangent, weight_one, weight_two):
    scale = float(MB * NH * W) ** (-0.5)
    pre = conv_forward(features, weight_one)
    hidden = jax.nn.silu(pre).astype(jnp.bfloat16)
    block_out = (features.astype(jnp.float32) + conv_forward(hidden, weight_two)).astype(jnp.bfloat16)
    hidden_grad = conv_transpose(cotangent, weight_two)
    sigma = jax.nn.sigmoid(pre)
    slope = (hidden_grad * sigma * (1.0 + pre * (1.0 - sigma))).astype(jnp.bfloat16)
    input_grad = (cotangent.astype(jnp.float32) + conv_transpose(slope, weight_one)).astype(jnp.bfloat16)
    grad_one = kernel_grad(features, slope) * scale
    grad_two = kernel_grad(hidden, cotangent) * scale
    return (block_out, input_grad, grad_one, grad_two)
```

```python
import functools

import jax
import jax.numpy as jnp
from jax import lax
from jax.experimental import pallas as pl
from jax.experimental.pallas import tpu as pltpu
from jax.sharding import PartitionSpec as P

MESH = pl.DeviceIdType.MESH


def reversed_bits(value, width):
    out = 0
    for _ in range(width):
        out, value = out * 2 + value % 2, value // 2
    return out


def kernel(
    n, rows, cols, scale,
    x_ref, c_ref, before_ref, after_ref, w1_ref, w1t_ref, w2_ref, w2t_ref,
    out_ref, ingrad_ref, g_ref,
    sx, sc, sh, ss, deriv, acc, sent, got, send_sem, recv_sem,
):
    ch = x_ref.shape[1]
    stages = n.bit_length() - 1
    rc = ch // n
    me = lax.axis_index("tile")

    def bit_of(k):
        return (me // (1 << k)) % 2

    def partner_of(k):
        return me + (1 - 2 * bit_of(k)) * (1 << k)

    barrier = pltpu.get_barrier_semaphore()
    for k in range(stages):
        pl.semaphore_signal(barrier, inc=1, device_id={"tile": partner_of(k)}, device_id_type=MESH)

    def start_of(k):
        at = 0
        for m in range(k):
            at = at + bit_of(m) * (n >> (m + 1))
        return at

    def copy_of(g, k):
        half, off = n >> (k + 1), n - (n >> k)
        return pltpu.make_async_remote_copy(
            src_ref=sent.at[g, pl.ds(off, half)],
            dst_ref=got.at[g, pl.ds(off, half)],
            send_sem=send_sem.at[g, k],
            recv_sem=recv_sem.at[g, k],
            device_id={"tile": partner_of(k)},
            device_id_type=MESH,
        )

    def send(g, k):
        half, off = n >> (k + 1), n - (n >> k)
        base = start_of(k) + (1 - bit_of(k)) * half

        def step(p, carry):
            sent[g, off + p] = acc[g, base + p].astype(jnp.bfloat16)
            return carry

        lax.fori_loop(0, half, step, 0)
        copy_of(g, k).start()

    def receive(g, k):
        half, off = n >> (k + 1), n - (n >> k)
        base = start_of(k + 1)
        copy_of(g, k).wait()

        def step(p, carry):
            acc[g, base + p] = acc[g, base + p] + got[g, off + p].astype(jnp.float32)
            return carry

        lax.fori_loop(0, half, step, 0)

    def advance(g, k):
        receive(g, k)
        if k + 1 < stages:
            send(g, k + 1)
        else:
            g_ref[g] = acc[g, start_of(stages)]

    column = lax.broadcasted_iota(jnp.int32, (cols, ch), 0)

    def put_sides(dst, at, row):
        wide = row.astype(jnp.float32)
        left = jnp.where(column == 0, 0.0, pltpu.roll(wide, 1, 0))
        right = jnp.where(column == cols - 1, 0.0, pltpu.roll(wide, cols - 1, 0))
        dst[pl.ds(at, cols), 0:ch] = left.astype(jnp.bfloat16)
        dst[pl.ds(at, cols), 2 * ch : 3 * ch] = right.astype(jnp.bfloat16)

    def put(dst, at, row):
        dst[pl.ds(at, cols), ch : 2 * ch] = row
        put_sides(dst, at, row)

    def fill(dst, src, place):
        for r in range(2):
            put(dst, r * cols, before_ref[place + r])
            put(dst, (rows + 2 + r) * cols, after_ref[place + r])

        def step(r, carry):
            at = pl.multiple_of(r * cols, cols)
            put(dst, at + 2 * cols, src[pl.ds(at, cols), :])
            return carry

        lax.fori_loop(0, rows, step, 0)

    def fill_sides(dst):
        def step(r, carry):
            at = pl.multiple_of(r * cols, cols)
            put_sides(dst, at, dst[pl.ds(at, cols), ch : 2 * ch])
            return carry

        lax.fori_loop(0, rows + 2, step, 0)

    def conv(src, at, count, weight):
        total = None
        for a in range(3):
            term = jnp.dot(
                src[(at + a) * cols : (at + a + count) * cols, :],
                weight[a],
                preferred_element_type=jnp.float32,
            )
            total = term if total is None else total + term
        return total

    def kernel_term(g, left, src, at):
        for a in range(3):
            term = scale * jnp.dot(
                left,
                src[(at + a) * cols : (at + a + rows) * cols, :],
                preferred_element_type=jnp.float32,
            )
            for j in range(3):
                for chunk in range(n):
                    acc[g, reversed_bits(chunk, stages), 8 - (3 * a + j)] = term[
                        chunk * rc : (chunk + 1) * rc, j * ch : (j + 1) * ch
                    ]

    half_ext, half_own = (rows + 2) // 2, rows // 2
    top = jnp.where(me == 0, 0.0, 1.0)
    bottom = jnp.where(me == n - 1, 0.0, 1.0)

    fill(sx, x_ref, 0)
    for part in range(2):
        count = half_ext if part == 0 else rows + 2 - half_ext
        lo = part * half_ext
        pre = conv(sx, lo, count, w1_ref)
        sig = 1.0 / (1.0 + jnp.exp(-pre))
        hid = (pre * sig).astype(jnp.bfloat16)
        sh[lo * cols : (lo + count) * cols, ch : 2 * ch] = hid
        deriv[lo * cols : (lo + count) * cols, :] = sig * (1.0 + pre * (1.0 - sig))
    last = (rows + 1) * cols
    for at, keep in ((0, top), (last, bottom)):
        edge = sh[at : at + cols, ch : 2 * ch].astype(jnp.float32) * keep
        sh[at : at + cols, ch : 2 * ch] = edge.astype(jnp.bfloat16)
        deriv[at : at + cols, :] = deriv[at : at + cols, :] * keep

    fill(sc, c_ref, 2)
    kernel_term(1, sh[cols : (rows + 1) * cols, ch : 2 * ch].T, sc, 1)
    pl.semaphore_wait(barrier, stages)
    send(1, 0)

    for part in range(2):
        count = half_ext if part == 0 else rows + 2 - half_ext
        lo = part * half_ext
        grad = conv(sc, lo, count, w2t_ref)
        ss[lo * cols : (lo + count) * cols, ch : 2 * ch] = (
            grad * deriv[lo * cols : (lo + count) * cols, :]
        ).astype(jnp.bfloat16)
        if part == 0:
            advance(1, 0)
    fill_sides(ss)
    kernel_term(0, x_ref[...].T, ss, 0)
    send(0, 0)
    if stages > 1:
        advance(1, 1)

    fill_sides(sh)
    done = {0: 0, 1: min(2, stages)}

    def move(g):
        if done[g] < stages:
            advance(g, done[g])
            done[g] += 1

    for part in range(2):
        rs = slice(part * half_own * cols, (part + 1) * half_own * cols)
        total = conv(sh, part * half_own, half_own, w2_ref)
        out_ref[rs, :] = (x_ref[rs, :].astype(jnp.float32) + total).astype(jnp.bfloat16)
        move(0)
        move(1)
    for part in range(2):
        rs = slice(part * half_own * cols, (part + 1) * half_own * cols)
        total = conv(ss, part * half_own, half_own, w1t_ref)
        ingrad_ref[rs, :] = (c_ref[rs, :].astype(jnp.float32) + total).astype(jnp.bfloat16)
        move(0)
        move(1)
    for _ in range(stages):
        move(1)
        move(0)


def body(features, cotangent, weight_one, weight_two):
    batch, rows, cols, ch = features.shape
    n = lax.axis_size("tile")
    stages = n.bit_length() - 1
    scale = float(batch * rows * n * cols) ** (-0.5)
    up = [(i, i + 1) for i in range(n - 1)]
    down = [(j, i) for i, j in up]
    x, c = features[0], cotangent[0]
    before = lax.ppermute(jnp.concatenate([x[-2:], c[-2:]]), "tile", up)
    after = lax.ppermute(jnp.concatenate([x[:2], c[:2]]), "tile", down)

    def straight(w):
        return jnp.transpose(w, (1, 0, 2)).reshape(3, 3 * ch, ch)

    def turned(w):
        return jnp.flip(jnp.transpose(w, (1, 2, 0)), 0).reshape(3, 3 * ch, ch)

    flat = (rows * cols, ch)
    rc = ch // n
    bf, f32 = jnp.bfloat16, jnp.float32
    vm = pl.BlockSpec(memory_space=pltpu.VMEM)
    out, ingrad, grads = pl.pallas_call(
        functools.partial(kernel, n, rows, cols, scale),
        out_shape=(
            jax.ShapeDtypeStruct(flat, bf),
            jax.ShapeDtypeStruct(flat, bf),
            jax.ShapeDtypeStruct((2, 9, rc, ch), f32),
        ),
        in_specs=[vm] * 8,
        out_specs=(vm, vm, vm),
        scratch_shapes=[
            pltpu.VMEM(((rows + 4) * cols, 3 * ch), bf),
            pltpu.VMEM(((rows + 4) * cols, 3 * ch), bf),
            pltpu.VMEM(((rows + 2) * cols, 3 * ch), bf),
            pltpu.VMEM(((rows + 2) * cols, 3 * ch), bf),
            pltpu.VMEM(((rows + 2) * cols, ch), f32),
            pltpu.VMEM((2, n, 9, rc, ch), f32),
            pltpu.VMEM((2, n - 1, 9, rc, ch), bf),
            pltpu.VMEM((2, n - 1, 9, rc, ch), bf),
            pltpu.SemaphoreType.DMA((2, stages)),
            pltpu.SemaphoreType.DMA((2, stages)),
        ],
        compiler_params=pltpu.CompilerParams(
            collective_id=0, has_side_effects=True, vmem_limit_bytes=56 * 1024 * 1024
        ),
        cost_estimate=pl.CostEstimate(
            flops=6 * 18 * rows * cols * ch * ch, bytes_accessed=16 * 1024 * 1024, transcendentals=rows * cols * ch
        ),
    )(
        x.reshape(flat), c.reshape(flat), before, after,
        straight(weight_one), turned(weight_one), straight(weight_two), turned(weight_two),
    )
    grads = jnp.transpose(grads, (0, 2, 1, 3))
    return (out.reshape(features.shape), ingrad.reshape(features.shape), grads[0], grads[1])


def solution(mesh):
    in_specs = (P("groups", "tile", None, None), P("groups", "tile", None, None), P(), P())
    out_specs = (
        P("groups", "tile", None, None),
        P("groups", "tile", None, None),
        P("tile", "groups", None),
        P("tile", "groups", None),
    )
    return jax.shard_map(body, mesh=mesh, in_specs=in_specs, out_specs=out_specs, check_vma=False)
```

```python
import functools

import jax
import jax.numpy as jnp
from jax import lax
from jax.experimental import pallas as pl
from jax.experimental.pallas import tpu as pltpu
from jax.sharding import PartitionSpec as P

MESH = pl.DeviceIdType.MESH


def position(chunk, order):
    out = 0
    for bit in order:
        out = out * 2 + (chunk >> bit) % 2
    return out


def kernel(
    n, rows, cols, scale,
    x_ref, c_ref, w1_ref, w2_ref,
    out_ref, ingrad_ref, g1_ref, g2_ref,
    w1t_ref, w2t_ref, sx, sc, sh, ss, deriv, before_ref, after_ref, acc, got_wide, sent, got,
    edge_send, edge_recv, send_sem, recv_sem,
):
    ch = x_ref.shape[1]
    stages = n.bit_length() - 1
    rc = ch // n
    me = lax.axis_index("tile")
    plain = list(range(stages))
    turned = plain[:1] + plain[2:] + plain[1:2]
    orders = (plain, turned, plain)

    def bit_of(bit):
        return (me // (1 << bit)) % 2

    def partner_of(bit):
        return me + (1 - 2 * bit_of(bit)) * (1 << bit)

    barrier = pltpu.get_barrier_semaphore()
    for k in range(stages):
        pl.semaphore_signal(barrier, inc=1, device_id={"tile": partner_of(k)}, device_id_type=MESH)

    @pl.when(me > 0)
    def _():
        pl.semaphore_signal(barrier, inc=1, device_id={"tile": me - 1}, device_id_type=MESH)

    @pl.when(me < n - 1)
    def _():
        pl.semaphore_signal(barrier, inc=1, device_id={"tile": me + 1}, device_id_type=MESH)

    neighbours = jnp.where(me > 0, 1, 0) + jnp.where(me < n - 1, 1, 0)
    pl.semaphore_wait(barrier, stages + neighbours)

    two = 2 * cols

    def edge_up(f):
        src = (x_ref, c_ref)[f]
        return pltpu.make_async_remote_copy(
            src_ref=src.at[pl.ds((rows - 2) * cols, two)],
            dst_ref=before_ref.at[f],
            send_sem=edge_send.at[0, f],
            recv_sem=edge_recv.at[0, f],
            device_id={"tile": me + 1},
            device_id_type=MESH,
        )

    def edge_down(f):
        src = (x_ref, c_ref)[f]
        return pltpu.make_async_remote_copy(
            src_ref=src.at[pl.ds(0, two)],
            dst_ref=after_ref.at[f],
            send_sem=edge_send.at[1, f],
            recv_sem=edge_recv.at[1, f],
            device_id={"tile": me - 1},
            device_id_type=MESH,
        )

    for f in range(2):
        @pl.when(me < n - 1)
        def _():
            edge_up(f).start()

        @pl.when(me > 0)
        def _():
            edge_down(f).start()

    def edges_arrive(f):
        @pl.when(me > 0)
        def _():
            edge_up(f).wait_recv()

        @pl.when(me < n - 1)
        def _():
            edge_down(f).wait_recv()

        @pl.when(me == 0)
        def _():
            before_ref[f] = jnp.zeros((two, ch), jnp.bfloat16)

        @pl.when(me == n - 1)
        def _():
            after_ref[f] = jnp.zeros((two, ch), jnp.bfloat16)

    def start_of(a, k):
        at = 0
        for m in range(k):
            at = at + bit_of(orders[a][m]) * (n >> (m + 1))
        return at

    def copy_of(g, a, k):
        half, off = n >> (k + 1), n // 2 - (n >> k)
        if k == 0:
            src = acc.at[g, a, pl.ds((1 - bit_of(orders[a][0])) * half, half)]
            dst = got_wide.at[g, a]
        else:
            src = sent.at[g, a, pl.ds(off, half)]
            dst = got.at[g, a, pl.ds(off, half)]
        return pltpu.make_async_remote_copy(
            src_ref=src,
            dst_ref=dst,
            send_sem=send_sem.at[g, a, k],
            recv_sem=recv_sem.at[g, a, k],
            device_id={"tile": partner_of(orders[a][k])},
            device_id_type=MESH,
        )

    def send(g, a, k):
        half, off = n >> (k + 1), n // 2 - (n >> k)
        if k > 0:
            base = start_of(a, k) + (1 - bit_of(orders[a][k])) * half

            def step(p, carry):
                sent[g, a, off + p] = acc[g, a, base + p].astype(jnp.bfloat16)
                return carry

            lax.fori_loop(0, half, step, 0)
        copy_of(g, a, k).start()

    def receive(g, a, k):
        half, off = n >> (k + 1), n // 2 - (n >> k)
        base = start_of(a, k + 1)
        copy_of(g, a, k).wait()

        def step(p, carry):
            term = got_wide[g, a, p] if k == 0 else got[g, a, off + p].astype(jnp.float32)
            acc[g, a, base + p] = acc[g, a, base + p] + term
            return carry

        lax.fori_loop(0, half, step, 0)

    done = {}

    def move(g):
        for a in range(3):
            k = done[g, a]
            if k < stages:
                receive(g, a, k)
                done[g, a] = k + 1
                if k + 1 < stages:
                    send(g, a, k + 1)
                else:
                    last = acc[g, a, start_of(a, stages)]
                    for j in range(3):
                        (g1_ref, g2_ref)[g][8 - (3 * a + j)] = last[j]

    column = lax.broadcasted_iota(jnp.int32, (cols, ch), 0)

    def put_sides(dst, at, row):
        wide = row.astype(jnp.float32)
        left = jnp.where(column == 0, 0.0, pltpu.roll(wide, 1, 0))
        right = jnp.where(column == cols - 1, 0.0, pltpu.roll(wide, cols - 1, 0))
        dst[pl.ds(at, cols), 0:ch] = left.astype(jnp.bfloat16)
        dst[pl.ds(at, cols), 2 * ch : 3 * ch] = right.astype(jnp.bfloat16)

    def put(dst, at, row):
        dst[pl.ds(at, cols), ch : 2 * ch] = row
        put_sides(dst, at, row)

    def fill(dst, src, place):
        def step(r, carry):
            at = pl.multiple_of(r * cols, cols)
            put(dst, at + 2 * cols, src[pl.ds(at, cols), :])
            return carry

        lax.fori_loop(0, rows, step, 0)
        edges_arrive(place)
        for r in range(2):
            put(dst, r * cols, before_ref[place, r * cols : (r + 1) * cols, :])
            put(dst, (rows + 2 + r) * cols, after_ref[place, r * cols : (r + 1) * cols, :])

    def fill_sides(dst):
        def step(r, carry):
            at = pl.multiple_of(r * cols, cols)
            put_sides(dst, at, dst[pl.ds(at, cols), ch : 2 * ch])
            return carry

        lax.fori_loop(0, rows + 2, step, 0)

    def conv(src, at, count, weight):
        total = None
        for a in range(3):
            term = jnp.dot(
                src[(at + a) * cols : (at + a + count) * cols, :],
                weight[a],
                preferred_element_type=jnp.float32,
            )
            total = term if total is None else total + term
        return total

    def kernel_term(g, left, src, at, between=None):
        for a in range(3):
            term = scale * jnp.dot(
                left,
                src[(at + a) * cols : (at + a + rows) * cols, :],
                preferred_element_type=jnp.float32,
            )
            for j in range(3):
                for chunk in range(n):
                    acc[g, a, position(chunk, orders[a]), j] = term[
                        chunk * rc : (chunk + 1) * rc, j * ch : (j + 1) * ch
                    ]
            send(g, a, 0)
            done[g, a] = 0
            if between is not None and a == 1:
                between()

    half_ext, half_own = (rows + 2) // 2, rows // 2
    top = jnp.where(me == 0, 0.0, 1.0)
    bottom = jnp.where(me == n - 1, 0.0, 1.0)

    for dst, src in ((w2t_ref, w2_ref), (w1t_ref, w1_ref)):
        for a in range(3):
            for j in range(3):
                dst[a, j * ch : (j + 1) * ch, :] = src[2 - a, (2 - j) * ch : (3 - j) * ch, :].T

    fill(sx, x_ref, 0)
    for part in range(2):
        count = half_ext if part == 0 else rows + 2 - half_ext
        lo = part * half_ext
        pre = conv(sx, lo, count, w1_ref)
        sig = 1.0 / (1.0 + jnp.exp(-pre))
        hid = (pre * sig).astype(jnp.bfloat16)
        sh[lo * cols : (lo + count) * cols, ch : 2 * ch] = hid
        deriv[lo * cols : (lo + count) * cols, :] = sig * (1.0 + pre * (1.0 - sig))
    last = (rows + 1) * cols
    for at, keep in ((0, top), (last, bottom)):
        edge = sh[at : at + cols, ch : 2 * ch].astype(jnp.float32) * keep
        sh[at : at + cols, ch : 2 * ch] = edge.astype(jnp.bfloat16)
        deriv[at : at + cols, :] = deriv[at : at + cols, :] * keep

    fill(sc, c_ref, 1)
    kernel_term(1, sh[cols : (rows + 1) * cols, ch : 2 * ch].T, sc, 1)

    for part in range(2):
        count = half_ext if part == 0 else rows + 2 - half_ext
        lo = part * half_ext
        grad = conv(sc, lo, count, w2t_ref)
        ss[lo * cols : (lo + count) * cols, ch : 2 * ch] = (
            grad * deriv[lo * cols : (lo + count) * cols, :]
        ).astype(jnp.bfloat16)
        if part == 0:
            move(1)
    fill_sides(ss)
    kernel_term(0, x_ref[...].T, ss, 0, lambda: move(1))

    fill_sides(sh)
    move(0)
    for part in range(2):
        rs = slice(part * half_own * cols, (part + 1) * half_own * cols)
        total = conv(sh, part * half_own, half_own, w2_ref)
        out_ref[rs, :] = (x_ref[rs, :].astype(jnp.float32) + total).astype(jnp.bfloat16)
        move(1 - part)
    for part in range(2):
        rs = slice(part * half_own * cols, (part + 1) * half_own * cols)
        total = conv(ss, part * half_own, half_own, w1t_ref)
        ingrad_ref[rs, :] = (c_ref[rs, :].astype(jnp.float32) + total).astype(jnp.bfloat16)
        move(1 - part)
    for _ in range(stages):
        move(0)
        move(1)
    for f in range(2):
        @pl.when(me < n - 1)
        def _():
            edge_up(f).wait_send()

        @pl.when(me > 0)
        def _():
            edge_down(f).wait_send()


def body(features, cotangent, weight_one, weight_two):
    batch, rows, cols, ch = features.shape
    n = lax.axis_size("tile")
    stages = n.bit_length() - 1
    scale = float(batch * rows * n * cols) ** (-0.5)
    x, c = features[0], cotangent[0]

    def straight(w):
        return jnp.transpose(w, (1, 0, 2)).reshape(3, 3 * ch, ch)

    flat = (rows * cols, ch)
    rc = ch // n
    bf, f32 = jnp.bfloat16, jnp.float32
    vm = pl.BlockSpec(memory_space=pltpu.VMEM)
    out, ingrad, grad_one, grad_two = pl.pallas_call(
        functools.partial(kernel, n, rows, cols, scale),
        out_shape=(
            jax.ShapeDtypeStruct(flat, bf),
            jax.ShapeDtypeStruct(flat, bf),
            jax.ShapeDtypeStruct((9, rc, ch), f32),
            jax.ShapeDtypeStruct((9, rc, ch), f32),
        ),
        in_specs=[vm] * 4,
        out_specs=(vm, vm, vm, vm),
        scratch_shapes=[
            pltpu.VMEM((3, 3 * ch, ch), bf),
            pltpu.VMEM((3, 3 * ch, ch), bf),
            pltpu.VMEM(((rows + 4) * cols, 3 * ch), bf),
            pltpu.VMEM(((rows + 4) * cols, 3 * ch), bf),
            pltpu.VMEM(((rows + 2) * cols, 3 * ch), bf),
            pltpu.VMEM(((rows + 2) * cols, 3 * ch), bf),
            pltpu.VMEM(((rows + 2) * cols, ch), f32),
            pltpu.VMEM((2, 2 * cols, ch), bf),
            pltpu.VMEM((2, 2 * cols, ch), bf),
            pltpu.VMEM((2, 3, n, 3, rc, ch), f32),
            pltpu.VMEM((2, 3, n // 2, 3, rc, ch), f32),
            pltpu.VMEM((2, 3, max(n // 2 - 1, 1), 3, rc, ch), bf),
            pltpu.VMEM((2, 3, max(n // 2 - 1, 1), 3, rc, ch), bf),
            pltpu.SemaphoreType.DMA((2, 2)),
            pltpu.SemaphoreType.DMA((2, 2)),
            pltpu.SemaphoreType.DMA((2, 3, stages)),
            pltpu.SemaphoreType.DMA((2, 3, stages)),
        ],
        compiler_params=pltpu.CompilerParams(
            collective_id=0, has_side_effects=True, vmem_limit_bytes=56 * 1024 * 1024
        ),
        cost_estimate=pl.CostEstimate(
            flops=6 * 18 * rows * cols * ch * ch, bytes_accessed=16 * 1024 * 1024, transcendentals=rows * cols * ch
        ),
    )(
        x.reshape(flat), c.reshape(flat),
        straight(weight_one), straight(weight_two),
    )
    return (out.reshape(features.shape), ingrad.reshape(features.shape), jnp.transpose(grad_one, (1, 0, 2)), jnp.transpose(grad_two, (1, 0, 2)))


def solution(mesh):
    in_specs = (P("groups", "tile", None, None), P("groups", "tile", None, None), P(), P())
    out_specs = (
        P("groups", "tile", None, None),
        P("groups", "tile", None, None),
        P("tile", "groups", None),
        P("tile", "groups", None),
    )
    return jax.shard_map(body, mesh=mesh, in_specs=in_specs, out_specs=out_specs, check_vma=False)
```

```python
import functools

import jax
import jax.numpy as jnp
from jax import lax
from jax.experimental import pallas as pl
from jax.experimental.pallas import tpu as pltpu
from jax.sharding import PartitionSpec as P

MESH = pl.DeviceIdType.MESH


def position(chunk, order):
    out = 0
    for bit in order:
        out = out * 2 + (chunk >> bit) % 2
    return out


def kernel(
    n, rows, cols, scale,
    x_ref, c_ref, w1_ref, w2_ref,
    out_ref, ingrad_ref, g1_ref, g2_ref,
    w1t_ref, w2t_ref, sx, sc, sh, ss, deriv, before_ref, after_ref, acc, got_wide, sent, got,
    edge_send, edge_recv, send_sem, recv_sem,
):
    ch = x_ref.shape[1]
    stages = n.bit_length() - 1
    rc = ch // n
    me = lax.axis_index("tile")
    plain = list(range(stages))
    turned = plain[:1] + plain[2:] + plain[1:2]
    orders = (plain, turned, plain)

    def bit_of(bit):
        return (me // (1 << bit)) % 2

    def partner_of(bit):
        return me + (1 - 2 * bit_of(bit)) * (1 << bit)

    barrier = pltpu.get_barrier_semaphore()
    for k in range(stages):
        pl.semaphore_signal(barrier, inc=1, device_id={"tile": partner_of(k)}, device_id_type=MESH)

    @pl.when(me > 0)
    def _():
        pl.semaphore_signal(barrier, inc=1, device_id={"tile": me - 1}, device_id_type=MESH)

    @pl.when(me < n - 1)
    def _():
        pl.semaphore_signal(barrier, inc=1, device_id={"tile": me + 1}, device_id_type=MESH)

    neighbours = jnp.where(me > 0, 1, 0) + jnp.where(me < n - 1, 1, 0)
    pl.semaphore_wait(barrier, stages + neighbours)

    two = 2 * cols

    def edge_up(f):
        src = (x_ref, c_ref)[f]
        return pltpu.make_async_remote_copy(
            src_ref=src.at[pl.ds((rows - 2) * cols, two)],
            dst_ref=before_ref.at[f],
            send_sem=edge_send.at[0, f],
            recv_sem=edge_recv.at[0, f],
            device_id={"tile": me + 1},
            device_id_type=MESH,
        )

    def edge_down(f):
        src = (x_ref, c_ref)[f]
        return pltpu.make_async_remote_copy(
            src_ref=src.at[pl.ds(0, two)],
            dst_ref=after_ref.at[f],
            send_sem=edge_send.at[1, f],
            recv_sem=edge_recv.at[1, f],
            device_id={"tile": me - 1},
            device_id_type=MESH,
        )

    for f in range(2):
        @pl.when(me < n - 1)
        def _():
            edge_up(f).start()

        @pl.when(me > 0)
        def _():
            edge_down(f).start()

    def edges_arrive(f):
        @pl.when(me > 0)
        def _():
            edge_up(f).wait_recv()

        @pl.when(me < n - 1)
        def _():
            edge_down(f).wait_recv()

        @pl.when(me == 0)
        def _():
            before_ref[f] = jnp.zeros((two, ch), jnp.bfloat16)

        @pl.when(me == n - 1)
        def _():
            after_ref[f] = jnp.zeros((two, ch), jnp.bfloat16)

    def start_of(a, k):
        at = 0
        for m in range(k):
            at = at + bit_of(orders[a][m]) * (n >> (m + 1))
        return at

    def copy_of(g, a, k):
        half, off = n >> (k + 1), n // 2 - (n >> k)
        if k == 0:
            src = acc.at[g, a, pl.ds((1 - bit_of(orders[a][0])) * half, half)]
            dst = got_wide.at[g, a]
        else:
            src = sent.at[g, a, pl.ds(off, half)]
            dst = got.at[g, a, pl.ds(off, half)]
        return pltpu.make_async_remote_copy(
            src_ref=src,
            dst_ref=dst,
            send_sem=send_sem.at[g, a, k],
            recv_sem=recv_sem.at[g, a, k],
            device_id={"tile": partner_of(orders[a][k])},
            device_id_type=MESH,
        )

    def send(g, a, k):
        half, off = n >> (k + 1), n // 2 - (n >> k)
        if k > 0:
            base = start_of(a, k) + (1 - bit_of(orders[a][k])) * half

            def step(p, carry):
                sent[g, a, off + p] = acc[g, a, base + p].astype(jnp.bfloat16)
                return carry

            lax.fori_loop(0, half, step, 0)
        copy_of(g, a, k).start()

    def receive(g, a, k):
        half, off = n >> (k + 1), n // 2 - (n >> k)
        base = start_of(a, k + 1)
        copy_of(g, a, k).wait()

        def step(p, carry):
            term = got_wide[g, a, p] if k == 0 else got[g, a, off + p].astype(jnp.float32)
            acc[g, a, base + p] = acc[g, a, base + p] + term
            return carry

        lax.fori_loop(0, half, step, 0)

    done = {}

    def move(g):
        for a in range(3):
            k = done[g, a]
            if k < stages:
                receive(g, a, k)
                done[g, a] = k + 1
                if k + 1 < stages:
                    send(g, a, k + 1)
                else:
                    last = acc[g, a, start_of(a, stages)]
                    for j in range(3):
                        (g1_ref, g2_ref)[g][8 - (3 * a + j)] = last[j]

    column = lax.broadcasted_iota(jnp.int32, (cols, ch), 0)

    def put_sides(dst, at, row):
        wide = row.astype(jnp.float32)
        left = jnp.where(column == 0, 0.0, pltpu.roll(wide, 1, 0))
        right = jnp.where(column == cols - 1, 0.0, pltpu.roll(wide, cols - 1, 0))
        dst[pl.ds(at, cols), 0:ch] = left.astype(jnp.bfloat16)
        dst[pl.ds(at, cols), 2 * ch : 3 * ch] = right.astype(jnp.bfloat16)

    def put(dst, at, row):
        dst[pl.ds(at, cols), ch : 2 * ch] = row
        put_sides(dst, at, row)

    def fill(dst, src, place):
        def step(r, carry):
            at = pl.multiple_of(r * cols, cols)
            put(dst, at + 2 * cols, src[pl.ds(at, cols), :])
            return carry

        lax.fori_loop(0, rows, step, 0)
        edges_arrive(place)
        for r in range(2):
            put(dst, r * cols, before_ref[place, r * cols : (r + 1) * cols, :])
            put(dst, (rows + 2 + r) * cols, after_ref[place, r * cols : (r + 1) * cols, :])

    def fill_sides(dst):
        def step(r, carry):
            at = pl.multiple_of(r * cols, cols)
            put_sides(dst, at, dst[pl.ds(at, cols), ch : 2 * ch])
            return carry

        lax.fori_loop(0, rows + 2, step, 0)

    def conv(src, at, count, weight):
        total = None
        for a in range(3):
            term = jnp.dot(
                src[(at + a) * cols : (at + a + count) * cols, :],
                weight[a],
                preferred_element_type=jnp.float32,
            )
            total = term if total is None else total + term
        return total

    def kernel_term(g, left, src, at, between=None):
        for a in range(3):
            term = scale * jnp.dot(
                left,
                src[(at + a) * cols : (at + a + rows) * cols, :],
                preferred_element_type=jnp.float32,
            )
            for j in range(3):
                for chunk in range(n):
                    acc[g, a, position(chunk, orders[a]), j] = term[
                        chunk * rc : (chunk + 1) * rc, j * ch : (j + 1) * ch
                    ]
            send(g, a, 0)
            done[g, a] = 0
            if between is not None and a == 1:
                between()

    half_ext, half_own = (rows + 2) // 2, rows // 2
    top = jnp.where(me == 0, 0.0, 1.0)
    bottom = jnp.where(me == n - 1, 0.0, 1.0)

    for dst, src in ((w2t_ref, w2_ref), (w1t_ref, w1_ref)):
        for a in range(3):
            for j in range(3):
                dst[a, j * ch : (j + 1) * ch, :] = src[2 - a, (2 - j) * ch : (3 - j) * ch, :].T

    fill(sx, x_ref, 0)
    for part in range(2):
        count = half_ext if part == 0 else rows + 2 - half_ext
        lo = part * half_ext
        pre = conv(sx, lo, count, w1_ref)
        sig = 1.0 / (1.0 + jnp.exp(-pre))
        hid = (pre * sig).astype(jnp.bfloat16)
        sh[lo * cols : (lo + count) * cols, ch : 2 * ch] = hid
        deriv[lo * cols : (lo + count) * cols, :] = sig * (1.0 + pre * (1.0 - sig))
    last = (rows + 1) * cols
    for at, keep in ((0, top), (last, bottom)):
        edge = sh[at : at + cols, ch : 2 * ch].astype(jnp.float32) * keep
        sh[at : at + cols, ch : 2 * ch] = edge.astype(jnp.bfloat16)
        deriv[at : at + cols, :] = deriv[at : at + cols, :] * keep

    fill(sc, c_ref, 1)
    kernel_term(1, sh[cols : (rows + 1) * cols, ch : 2 * ch].T, sc, 1)

    for part in range(2):
        count = half_ext if part == 0 else rows + 2 - half_ext
        lo = part * half_ext
        grad = conv(sc, lo, count, w2t_ref)
        ss[lo * cols : (lo + count) * cols, ch : 2 * ch] = (
            grad * deriv[lo * cols : (lo + count) * cols, :]
        ).astype(jnp.bfloat16)
        if part == 0:
            move(1)
    fill_sides(ss)
    kernel_term(0, x_ref[...].T, ss, 0, lambda: move(1))

    fill_sides(sh)
    move(0)
    for part in range(2):
        rs = slice(part * half_own * cols, (part + 1) * half_own * cols)
        total = conv(sh, part * half_own, half_own, w2_ref)
        out_ref[rs, :] = (x_ref[rs, :].astype(jnp.float32) + total).astype(jnp.bfloat16)
        move(1 - part)
    for part in range(2):
        rs = slice(part * half_own * cols, (part + 1) * half_own * cols)
        total = conv(ss, part * half_own, half_own, w1t_ref)
        ingrad_ref[rs, :] = (c_ref[rs, :].astype(jnp.float32) + total).astype(jnp.bfloat16)
        move(1 - part)
    for _ in range(stages):
        move(0)
        move(1)
    for f in range(2):
        @pl.when(me < n - 1)
        def _():
            edge_up(f).wait_send()

        @pl.when(me > 0)
        def _():
            edge_down(f).wait_send()


def hand_on(pieces, a_in, b_in, c_in, d_in, a_out, b_out, c_out, d_out, sems):
    copies = []
    for src, dst in ((a_in, a_out), (b_in, b_out)):
        size = src.shape[0] // pieces
        for at in range(pieces):
            rows = pl.ds(at * size, size)
            copies.append((src.at[rows], dst.at[rows]))
    copies += [(c_in, c_out), (d_in, d_out)]
    started = [pltpu.make_async_copy(s, d, sems.at[i]) for i, (s, d) in enumerate(copies)]
    for copy in started:
        copy.start()
    for copy in started:
        copy.wait()


def body(features, cotangent, weight_one, weight_two):
    batch, rows, cols, ch = features.shape
    n = lax.axis_size("tile")
    stages = n.bit_length() - 1
    scale = float(batch * rows * n * cols) ** (-0.5)
    x, c = features[0], cotangent[0]

    def straight(w):
        return jnp.transpose(w, (1, 0, 2)).reshape(3, 3 * ch, ch)

    flat = (rows * cols, ch)
    rc = ch // n
    bf, f32 = jnp.bfloat16, jnp.float32
    vm = pl.BlockSpec(memory_space=pltpu.VMEM)
    out, ingrad, grad_one, grad_two = pl.pallas_call(
        functools.partial(kernel, n, rows, cols, scale),
        out_shape=(
            jax.ShapeDtypeStruct(flat, bf),
            jax.ShapeDtypeStruct(flat, bf),
            jax.ShapeDtypeStruct((9, rc, ch), f32),
            jax.ShapeDtypeStruct((9, rc, ch), f32),
        ),
        in_specs=[vm] * 4,
        out_specs=(vm, vm, vm, vm),
        scratch_shapes=[
            pltpu.VMEM((3, 3 * ch, ch), bf),
            pltpu.VMEM((3, 3 * ch, ch), bf),
            pltpu.VMEM(((rows + 4) * cols, 3 * ch), bf),
            pltpu.VMEM(((rows + 4) * cols, 3 * ch), bf),
            pltpu.VMEM(((rows + 2) * cols, 3 * ch), bf),
            pltpu.VMEM(((rows + 2) * cols, 3 * ch), bf),
            pltpu.VMEM(((rows + 2) * cols, ch), f32),
            pltpu.VMEM((2, 2 * cols, ch), bf),
            pltpu.VMEM((2, 2 * cols, ch), bf),
            pltpu.VMEM((2, 3, n, 3, rc, ch), f32),
            pltpu.VMEM((2, 3, n // 2, 3, rc, ch), f32),
            pltpu.VMEM((2, 3, max(n // 2 - 1, 1), 3, rc, ch), bf),
            pltpu.VMEM((2, 3, max(n // 2 - 1, 1), 3, rc, ch), bf),
            pltpu.SemaphoreType.DMA((2, 2)),
            pltpu.SemaphoreType.DMA((2, 2)),
            pltpu.SemaphoreType.DMA((2, 3, stages)),
            pltpu.SemaphoreType.DMA((2, 3, stages)),
        ],
        compiler_params=pltpu.CompilerParams(
            collective_id=0, has_side_effects=True, vmem_limit_bytes=56 * 1024 * 1024
        ),
        cost_estimate=pl.CostEstimate(
            flops=6 * 18 * rows * cols * ch * ch, bytes_accessed=16 * 1024 * 1024, transcendentals=rows * cols * ch
        ),
    )(
        x.reshape(flat), c.reshape(flat),
        straight(weight_one), straight(weight_two),
    )
    anywhere = pl.BlockSpec(memory_space=pl.ANY)
    results = (out, ingrad, grad_one, grad_two)
    pieces = 4 if rows * cols % 64 == 0 else 1
    out, ingrad, grad_one, grad_two = pl.pallas_call(
        functools.partial(hand_on, pieces),
        out_shape=tuple(jax.ShapeDtypeStruct(r.shape, r.dtype) for r in results),
        in_specs=[anywhere] * 4,
        out_specs=(anywhere,) * 4,
        scratch_shapes=[pltpu.SemaphoreType.DMA((2 * pieces + 2,))],
        compiler_params=pltpu.CompilerParams(vmem_limit_bytes=56 * 1024 * 1024),
    )(*results)
    return (out.reshape(features.shape), ingrad.reshape(features.shape), jnp.transpose(grad_one, (1, 0, 2)), jnp.transpose(grad_two, (1, 0, 2)))


def solution(mesh):
    in_specs = (P("groups", "tile", None, None), P("groups", "tile", None, None), P(), P())
    out_specs = (
        P("groups", "tile", None, None),
        P("groups", "tile", None, None),
        P("tile", "groups", None),
        P("tile", "groups", None),
    )
    return jax.shard_map(body, mesh=mesh, in_specs=in_specs, out_specs=out_specs, check_vma=False)
```
